32 devices in a mesh: dp: 2 (over y), row: 2 (over core), col: 8 (over z, x).
Axes of the slice: x: 2, y: 2, z: 4, core: 2. Of those that a mesh axis runs over, the one named last changes fastest.
Arguments:
- activations: bfloat16 [2048, 16384], P(('dp', 'row'), 'col'), may hold values from -6 to 6
- cotangent: bfloat16 [2048, 16384], P(('dp', 'row'), 'col'), may hold values from -6 to 6
- gate_saved: bfloat16 [2048, 6656], P(('dp', 'col'), 'row'), may hold values from -6 to 6
- up_saved: bfloat16 [2048, 6656], P(('dp', 'col'), 'row'), may hold values from -6 to 6
- w_gate: bfloat16 [16384, 6656], P('col', 'row'), may hold values from -0.046875 to 0.046875
- w_up: bfloat16 [16384, 6656], P('col', 'row'), may hold values from -0.046875 to 0.046875
- w_down: bfloat16 [6656, 16384], P('row', 'col'), may hold values from -0.078125 to 0.078125
- assignment: int32 [4], replicated, may hold values from 0 to 3, each once
- pair_lengths: int32 [8], replicated, may hold values from 1 to 256, 1536 in all
Outputs:
- input_grad: bfloat16 [2048, 16384], P(('dp', 'row'), 'col')
- gate_grad: bfloat16 [16384, 6656], P(('col', 'dp'), 'row')
- up_grad: bfloat16 [16384, 6656], P(('col', 'dp'), 'row')
- down_grad: bfloat16 [6656, 16384], P(('row', 'dp'), 'col')
The draws below stay inside these ranges and needn't reach their ends.
Inputs may be any that keep to these rules, and one draw needn't show every extreme that they name: `assignment`: each of the 4 pairs stands in exactly one pair slot; pair slot s belongs to batch s // 2. `pair_lengths`: entry 2 p is the live length of pair p's chosen sequence and entry 2 p + 1 that of its rejected one; the largest entry is exactly 256.
All inputs are finite; a program needn't handle non-finite values.
Results may differ from the reference program's by a relative error of at most 0.019.
Values may be sent and summed in bfloat16 or wider, within the bound.
A program may use at most 192 MiB of HBM per device.

```python
import math
import jax
import jax.numpy as jnp
import numpy as np
from jax import lax

D = 16384
FF = 6656
SEQ = 256
TOK = 1024
PAIRS = 4
TOKENS = 2048
N_DP = 2
N_ROW = 2
N_COL = 8


def raised(array, rng, source, target, shards_of, factor):
    def block_of(dim):
        return (jnp.arange(array.shape[dim]) // (array.shape[dim] // shards_of)).reshape((-1,) + (1,) * (array.ndim - 1 - dim))

    first = jax.random.permutation(rng, shards_of)[block_of(target)]
    other_side = (block_of(target) + shards_of // 2) % shards_of
    return jnp.where((block_of(source) == first) | (block_of(source) == other_side), factor * array, array)


def shard_levels(stream_key, extent, cuts, least, largest):
    loudness = 1.0
    for dim, shards_of in cuts:
        draws = jax.random.uniform(jax.random.fold_in(jax.random.fold_in(stream_key, 6), dim), (shards_of,), jnp.float32, least / len(cuts), largest / len(cuts))
        loudness = loudness * jnp.repeat(jnp.exp(draws), extent[dim] // shards_of).reshape((-1,) + (1,) * (len(extent) - 1 - dim))
    return loudness


def profile(amount, total, limit, skew):
    weights = [(1 << 20) // math.isqrt(rank ** skew) + 1 for rank in range(2, amount + 1)]
    surplus, counts = total - limit - (amount - 1), [1] * (amount - 1)
    while surplus > 0:
        movable = [i for i in range(amount - 1) if counts[i] < limit]
        mass, budget = sum([weights[i] for i in movable]), surplus
        for i in movable:
            addition = min(limit - counts[i], max(1, budget * weights[i] // mass), surplus)
            counts[i] = counts[i] + addition
            surplus = surplus - addition
    return np.array([limit] + counts)


def ragged_sizes(stream_key, count, total, most, slope):
    if count == 2:
        one = jax.random.randint(stream_key, (), max(1, total - most), min(most, total - 1) + 1)
        return jnp.stack([one, total - one])
    lengths = jnp.asarray(profile(count, total, most, slope), jnp.int32)
    twos = (count - 1) // 2
    source_of, receiver = lengths[1:1 + 2 * twos:2], lengths[2:2 + 2 * twos:2]
    slack = jnp.minimum(source_of - 1, most - receiver)
    moved = jax.random.randint(jax.random.fold_in(stream_key, 1), (twos,), 0, 1 << 20) % (slack + 1)
    lengths = lengths.at[1:1 + 2 * twos:2].set(source_of - moved).at[2:2 + 2 * twos:2].set(receiver + moved)
    return lengths[jax.random.permutation(jax.random.fold_in(stream_key, 2), count)]


def gaussian(stream_key, shape, width, bound, pieces=(), kind=jnp.bfloat16):
    result = width * jax.random.normal(stream_key, shape, jnp.float32)
    if pieces:
        result = result * shard_levels(stream_key, shape, pieces, -0.22, 0.18)
    return jnp.clip(result, -bound, bound).astype(kind)


def bell_draw_with(key, dims, width, reach, pieces, heavy, kind=jnp.bfloat16):
    values = width * jax.random.normal(key, dims, jnp.float32)
    if pieces:
        values = values * shard_levels(key, dims, pieces, -0.22, 0.18)
    return jnp.clip(raised(values, jax.random.fold_in(key, 3), *heavy), -reach, reach).astype(kind)


def setup_inputs(seed: int = 0) -> dict:
    arg_keys = jax.random.split(jax.random.key(seed), 10)
    activations = bell_draw_with(arg_keys[0], (TOKENS, D), 1.0, 6.0, ((0, 4), (1, 8)), (0, 1, 8, 2.0))
    cotangent = bell_draw_with(arg_keys[1], (TOKENS, D), 1.0, 6.0, ((0, 4), (1, 8)), (1, 0, 8, 2.0))
    gate_saved = gaussian(arg_keys[2], (TOKENS, FF), 1.0, 6.0, ((0, 16), (1, 2)))
    up_saved = gaussian(arg_keys[3], (TOKENS, FF), 1.0, 6.0, ((0, 16), (1, 2)))
    w_gate = gaussian(arg_keys[4], (D, FF), D ** -0.5, 0.046875, ((0, 8), (1, 2)))
    w_up = gaussian(arg_keys[5], (D, FF), D ** -0.5, 0.046875, ((0, 8), (1, 2)))
    w_down = gaussian(arg_keys[6], (FF, D), FF ** -0.5, 0.078125, ((0, 2), (1, 8)))
    assignment = jax.random.permutation(arg_keys[7], PAIRS).astype(jnp.int32)
    pair_lengths = ragged_sizes(arg_keys[8], 2 * PAIRS, 3 * PAIRS * SEQ // 2, SEQ, 1).astype(jnp.int32)
    return dict(activations=activations, cotangent=cotangent, gate_saved=gate_saved, up_saved=up_saved, w_gate=w_gate, w_up=w_up, w_down=w_down, assignment=assignment, pair_lengths=pair_lengths)


def round_trip(values):
    return lax.optimization_barrier(values.astype(jnp.bfloat16)).astype(jnp.float32)

def contract_last(left, right):
    return lax.dot_general(left, right, (((1,), (1,)), ((), ())), preferred_element_type=jnp.float32)

def contract_first(left, right):
    return lax.dot_general(left, right, (((0,), (0,)), ((), ())), preferred_element_type=jnp.float32)

def reference(activations, cotangent, gate_saved, up_saved, w_gate, w_up, w_down, assignment, pair_lengths):
    position = jnp.arange(TOKENS, dtype=jnp.int32)
    slot_ids = position // (2 * SEQ)
    pair_ids = assignment[slot_ids]
    entry_ids = 2 * pair_ids + position // SEQ % 2
    live_tokens = position % SEQ < pair_lengths[entry_ids]
    masked = jnp.where(live_tokens[:, None], cotangent, jnp.zeros_like(cotangent))
    col_width = D // N_COL

    def head_block(total, index):
        start = index * col_width
        left = lax.dynamic_slice_in_dim(masked, start, col_width, 1)
        right = lax.dynamic_slice_in_dim(w_down, start, col_width, 1)
        return (total + round_trip(contract_last(left, right)), None)
    head_grad, _ = lax.scan(head_block, jnp.zeros((TOKENS, FF), jnp.float32), jnp.arange(N_COL, dtype=jnp.int32))
    gate_float = gate_saved.astype(jnp.float32)
    up_float = up_saved.astype(jnp.float32)
    sigmoid_gate = jax.nn.sigmoid(gate_float)
    silu_gate = gate_float * sigmoid_gate
    hidden = (silu_gate * up_float).astype(jnp.bfloat16)
    grad_gate = (head_grad * up_float * sigmoid_gate * (1.0 + gate_float * (1.0 - sigmoid_gate))).astype(jnp.bfloat16)
    grad_up = (head_grad * silu_gate).astype(jnp.bfloat16)
    row_width = FF // N_ROW

    def input_block(total, index):
        start = index * row_width
        left_gate = lax.dynamic_slice_in_dim(grad_gate, start, row_width, 1)
        left_up = lax.dynamic_slice_in_dim(grad_up, start, row_width, 1)
        right_gate = lax.dynamic_slice_in_dim(w_gate, start, row_width, 1)
        right_up = lax.dynamic_slice_in_dim(w_up, start, row_width, 1)
        term = contract_last(left_gate, right_gate) + contract_last(left_up, right_up)
        return (total + round_trip(term), None)
    input_sum, _ = lax.scan(input_block, jnp.zeros((TOKENS, D), jnp.float32), jnp.arange(N_ROW, dtype=jnp.int32))
    input_grad = input_sum.astype(jnp.bfloat16)
    grad_scale = 1.0 / jnp.sqrt(jnp.float32(TOKENS))
    gate_total = jnp.zeros((D, FF), jnp.float32)
    up_total = jnp.zeros((D, FF), jnp.float32)
    down_total = jnp.zeros((FF, D), jnp.float32)
    for batch_index in range(N_DP):
        first = batch_index * TOK
        last = first + TOK
        gate_total = gate_total + round_trip(contract_first(activations[first:last], grad_gate[first:last]) * grad_scale)
        up_total = up_total + round_trip(contract_first(activations[first:last], grad_up[first:last]) * grad_scale)
        down_total = down_total + round_trip(contract_first(hidden[first:last], masked[first:last]) * grad_scale)
    return (input_grad, gate_total.astype(jnp.bfloat16), up_total.astype(jnp.bfloat16), down_total.astype(jnp.bfloat16))
```

```python
import jax
import jax.numpy as jnp
from jax import lax
from jax.sharding import PartitionSpec as P

SEQ = 256
SHARES = (2, 3, 4, 4)


def contract_last(left, right):
    return lax.dot_general(
        left, right, (((1,), (1,)), ((), ())), preferred_element_type=jnp.float32
    )


def contract_first(left, right):
    return lax.dot_general(
        left, right, (((0,), (0,)), ((), ())), preferred_element_type=jnp.float32
    )


def cuts_of(size):
    whole = sum(SHARES)
    marks = [size * sum(SHARES[:i]) // whole for i in range(len(SHARES) + 1)]
    return list(zip(marks[:-1], marks[1:]))


def after(value, earlier):
    value, earlier = lax.optimization_barrier((value, earlier))
    return value, earlier


def placed(whole, piece, start):
    return lax.dynamic_update_slice_in_dim(whole, piece, start, 1)


def shifted(value, axis, shift):
    count = lax.axis_size(axis)
    return lax.ppermute(value, axis, [(i, (i + shift) % count) for i in range(count)])


def gather_rows(block, axis):
    count = lax.axis_size(axis)
    me = lax.axis_index(axis)
    rows = block.shape[0]
    whole = jnp.zeros((rows * count,) + block.shape[1:], block.dtype)
    whole = lax.dynamic_update_slice_in_dim(whole, block, me * rows, 0)
    for shift in range(1, count):
        source = (me - shift + count) % count
        whole = lax.dynamic_update_slice_in_dim(
            whole, shifted(block, axis, shift), source * rows, 0
        )
    return whole


def live_rows(assignment, pair_lengths, first, row_count):
    token = first + jnp.arange(row_count, dtype=jnp.int32)
    slot_table = jnp.arange(assignment.shape[0], dtype=jnp.int32)
    pair_ids = jnp.sum(
        jnp.where(slot_table[None, :] == (token // (2 * SEQ))[:, None], assignment[None, :], 0),
        axis=1,
    )
    entry_ids = 2 * pair_ids + token // SEQ % 2
    entry_table = jnp.arange(pair_lengths.shape[0], dtype=jnp.int32)
    live_len = jnp.sum(
        jnp.where(entry_table[None, :] == entry_ids[:, None], pair_lengths[None, :], 0), axis=1
    )
    return (token % SEQ < live_len)[:, None]


def on_device(
    activations, cotangent, gate_saved, up_saved, w_gate, w_up, w_down, assignment, pair_lengths
):
    dp_count, row_size, col_count = (
        lax.axis_size("dp"), lax.axis_size("row"), lax.axis_size("col"))
    dp, row, col = lax.axis_index("dp"), lax.axis_index("row"), lax.axis_index("col")
    bf16 = jnp.bfloat16
    shard_rows, ff = gate_saved.shape
    width = activations.shape[1]
    batch_rows = shard_rows * col_count
    scale = 1.0 / jnp.sqrt(jnp.float32(batch_rows * dp_count))
    live = live_rows(assignment, pair_lengths, (dp * col_count + col) * shard_rows, shard_rows)

    gate_float = gate_saved.astype(jnp.float32)
    up_float = up_saved.astype(jnp.float32)
    sig = jax.nn.sigmoid(gate_float)
    silu = gate_float * sig
    hidden = jnp.where(live, (silu * up_float), 0.0).astype(bf16)

    grads_batch = gather_rows(cotangent, "row")
    inputs_batch = gather_rows(activations, "row")

    half_ff = ff // dp_count
    hidden_parts = [lax.dynamic_slice_in_dim(hidden, dp * half_ff, half_ff, 1)]
    grads_all = [grads_batch]
    for shift in range(1, dp_count):
        target = (dp + shift) % dp_count
        hidden_parts.append(
            shifted(lax.dynamic_slice_in_dim(hidden, target * half_ff, half_ff, 1), "dp", shift)
        )
        grads_all.append(gather_rows(shifted(cotangent, "dp", shift), "row"))

    half_width = width // dp_count
    own_inputs = lax.dynamic_slice_in_dim(inputs_batch, dp * half_width, half_width, 1)
    far_inputs = [
        lax.dynamic_slice_in_dim(
            inputs_batch, ((dp + shift) % dp_count) * half_width, half_width, 1
        )
        for shift in range(1, dp_count)
    ]

    term = contract_last(grads_batch, w_down).astype(bf16)
    head = lax.psum_scatter(term, "col", scatter_dimension=0, tiled=True).astype(jnp.float32)
    head = jnp.where(live, head, 0.0)
    grad_gate = (head * up_float * sig * (1.0 + gate_float * (1.0 - sig))).astype(bf16)
    grad_up = (head * silu).astype(bf16)

    input_sum = None
    chunks = cuts_of(ff)
    gathered, far_terms, far_parts = [], [], []

    def send(index):
        far_parts[index:] = [
            [shifted(term, "dp", shift) for shift, term in enumerate(far_terms[index], 1)]
        ]

    for index, (low, high) in enumerate(chunks):
        pair = jnp.concatenate([grad_gate[:, low:high], grad_up[:, low:high]], axis=1)
        if index == 0:
            pair, (grads_all[1:], hidden_parts[1:], own_inputs, far_inputs) = after(
                pair, (grads_all[1:], hidden_parts[1:], own_inputs, far_inputs)
            )
        elif index == 1:
            pair, gathered[0] = after(pair, gathered[0])
        else:
            if index + 1 == len(chunks):
                pair, far_terms[-1] = after(pair, far_terms[-1])
                send(index - 1)
            pair, (gathered[-1], far_parts[index - 2]) = after(
                pair, (gathered[-1], far_parts[index - 2])
            )
        both = lax.all_gather(pair, "col", axis=0, tiled=True)
        gathered.append(both)
        far_terms.append(None)
        far_parts.append(None)
        far_terms[index] = [(contract_first(far, both) * scale).astype(bf16) for far in far_inputs]
        send(index)
    hidden_pair, gathered[-1] = after(jnp.concatenate(hidden_parts, axis=1), gathered[-1])
    far_terms[-1], far_parts[-2] = after(far_terms[-1], far_parts[-2])
    send(len(chunks) - 1)
    hidden_rows = lax.all_gather(hidden_pair, "col", axis=0, tiled=True)

    gate_grad = jnp.zeros((half_width, ff), bf16)
    up_grad = jnp.zeros((half_width, ff), bf16)
    for (low, high), both, parts in zip(chunks, gathered, far_parts):
        size = high - low
        gate_total = (contract_first(own_inputs, both[:, :size]) * scale).astype(bf16)
        up_total = (contract_first(own_inputs, both[:, size:]) * scale).astype(bf16)
        gate_total = gate_total.astype(jnp.float32)
        up_total = up_total.astype(jnp.float32)
        for part in parts:
            gate_total = gate_total + part[:, :size].astype(jnp.float32)
            up_total = up_total + part[:, size:].astype(jnp.float32)
        gate_grad = placed(gate_grad, gate_total.astype(bf16), low)
        up_grad = placed(up_grad, up_total.astype(bf16), low)
        piece = contract_last(both[:, :size], w_gate[:, low:high]) + contract_last(
            both[:, size:], w_up[:, low:high]
        )
        input_sum = piece if input_sum is None else input_sum + piece

    input_term = input_sum.astype(bf16)
    own_rows = activations.shape[0]
    input_grad = lax.dynamic_slice_in_dim(input_term, row * own_rows, own_rows, 0).astype(
        jnp.float32
    )
    for shift in range(1, row_size):
        target = (row + shift) % row_size
        part = lax.dynamic_slice_in_dim(input_term, target * own_rows, own_rows, 0)
        input_grad = input_grad + shifted(part, "row", shift).astype(jnp.float32)

    down = None
    for index, grads in enumerate(grads_all):
        rows = hidden_rows[:, index * half_ff : (index + 1) * half_ff]
        piece = (contract_first(rows, grads) * scale).astype(bf16).astype(jnp.float32)
        down = piece if down is None else down + piece

    return (
        input_grad.astype(bf16),
        gate_grad,
        up_grad,
        down.astype(bf16),
    )


def solution(mesh):
    return jax.shard_map(
        on_device,
        mesh=mesh,
        in_specs=(
            P(("dp", "row"), "col"),
            P(("dp", "row"), "col"),
            P(("dp", "col"), "row"),
            P(("dp", "col"), "row"),
            P("col", "row"),
            P("col", "row"),
            P("row", "col"),
            P(),
            P(),
        ),
        out_specs=(
            P(("dp", "row"), "col"),
            P(("col", "dp"), "row"),
            P(("col", "dp"), "row"),
            P(("row", "dp"), "col"),
        ),
        check_vma=False,
    )
```
